128 devices in a mesh: row: 32 (over y, z, core), col: 4 (over x).
Axes of the slice: x: 4, y: 4, z: 4, core: 2. Of those that a mesh axis runs over, the one named last changes fastest.
Arguments:
- hidden_in: bfloat16 [4096, 24576], P('row'), may hold values from -6 to 6
- down_weight: bfloat16 [24576, 6144], P('row', 'col'), may hold values from -0.0390625 to 0.0390625
- out_grad: bfloat16 [4096, 6144], P('row', 'col'), may hold values from -6 to 6
Outputs:
- ffn_out: bfloat16 [4096, 6144], P('row', 'col')
- hidden_grad: bfloat16 [4096, 24576], P('col', 'row')
- weight_grad: bfloat16 [24576, 6144], P('row', 'col')
The draws below stay inside these ranges and needn't reach their ends.
All inputs are finite; a program needn't handle non-finite values.
Results may differ from the reference program's by a relative error of at most 0.024.
Values may be sent and summed in bfloat16 or wider, within the bound.
No kernel may reach another device: no remote copies, remote signals or barrier semaphores. Data moves between devices by JAX's collectives and lax.ppermute only.
A program may use at most 128 MiB of HBM per device.

```python
import jax
import jax.numpy as jnp
from jax import lax

D = 6144
FF = 24576
TOKENS = 4096
PANEL = 768
COLS = 1536
N_ROW = 32
N_COL = 4


def block_scale(key, dims, split, smallest, high):
    def one(axis_at, parts):
        steps = jax.random.uniform(jax.random.fold_in(jax.random.fold_in(key, 6), axis_at), (parts,), jnp.float32, smallest / len(split), high / len(split))
        return jnp.repeat(jnp.exp(steps), dims[axis_at] // parts).reshape((-1,) + (1,) * (len(dims) - axis_at - 1))

    loudness = one(*split[0])
    for cut in split[1:]:
        loudness = loudness * one(*cut)
    return loudness


def gaussian(rng, shape, deviation, reach, pieces=(), dtype=jnp.bfloat16):
    drawn = jax.random.normal(rng, shape, jnp.float32) * deviation
    if len(pieces) > 0:
        drawn = block_scale(rng, shape, pieces, -0.22, 0.18) * drawn
    return jnp.clip(drawn, min=-reach, max=reach).astype(dtype)


def setup_inputs(seed: int = 0) -> dict:
    keys = jax.random.split(jax.random.key(seed), 4)
    return {
        "hidden_in": gaussian(keys[0], (TOKENS, FF), 1.0, 6.0, ((0, 32),)),
        "down_weight": gaussian(keys[1], (FF, D), FF ** -0.5, 0.0390625, ((0, 32), (1, 4))),
        "out_grad": gaussian(keys[2], (TOKENS, D), 1.0, 6.0, ((0, 32), (1, 4))),
    }


gelu_coeff = 0.7978845608
cubic_coeff = 0.044715


def gelu_value(inputs):
    inner = gelu_coeff * (inputs + cubic_coeff * inputs * inputs * inputs)
    return 0.5 * inputs * (1.0 + jnp.tanh(inner))


def gelu_slope(inputs):
    tanh_part = jnp.tanh(gelu_coeff * (inputs + cubic_coeff * inputs * inputs * inputs))
    return 0.5 * (1.0 + tanh_part) + 0.5 * inputs * (1.0 - tanh_part * tanh_part) * gelu_coeff * (1.0 + 3.0 * cubic_coeff * inputs * inputs)


def reference(hidden_in, down_weight, out_grad):
    activated = gelu_value(hidden_in.astype(jnp.float32)).astype(jnp.bfloat16)
    total_out = jnp.zeros((TOKENS, D), jnp.float32)
    for block_index in range(N_ROW):
        rows = activated[:, block_index * PANEL:(block_index + 1) * PANEL]
        weight_rows = down_weight[block_index * PANEL:(block_index + 1) * PANEL, :]
        part_sum = jnp.dot(rows, weight_rows, preferred_element_type=jnp.float32).astype(jnp.bfloat16)
        part_sum = lax.optimization_barrier(part_sum)
        total_out = total_out + part_sum.astype(jnp.float32)
    ffn_out = total_out.astype(jnp.bfloat16)
    back_total = jnp.zeros((TOKENS, FF), jnp.float32)
    for block_index in range(N_COL):
        grad_cols = out_grad[:, block_index * COLS:(block_index + 1) * COLS]
        weight_cols = down_weight[:, block_index * COLS:(block_index + 1) * COLS]
        back_part = lax.dot_general(grad_cols, weight_cols, (((1,), (1,)), ((), ())), preferred_element_type=jnp.float32).astype(jnp.bfloat16)
        back_part = lax.optimization_barrier(back_part)
        back_total = back_total + back_part.astype(jnp.float32)
    hidden_grad = (back_total * gelu_slope(hidden_in.astype(jnp.float32))).astype(jnp.bfloat16)
    weight_sum = lax.dot_general(activated, out_grad, (((0,), (0,)), ((), ())), preferred_element_type=jnp.float32)
    weight_grad = (weight_sum * (float(TOKENS) ** -0.5)).astype(jnp.bfloat16)
    return ffn_out, hidden_grad, weight_grad
```

```python
import jax
import jax.numpy as jnp
from jax import lax
from jax.experimental import pallas as pl
from jax.experimental.pallas import tpu as pltpu
from jax.sharding import Mesh, PartitionSpec as P

gelu_coeff = 0.7978845608
cubic_coeff = 0.044715


def gelu_value(inputs):
    inner = gelu_coeff * (inputs + cubic_coeff * inputs * inputs * inputs)
    return 0.5 * inputs * (1.0 + jnp.tanh(inner))


def gelu_slope(inputs):
    tanh_part = jnp.tanh(gelu_coeff * (inputs + cubic_coeff * inputs * inputs * inputs))
    return 0.5 * (1.0 + tanh_part) + 0.5 * inputs * (1.0 - tanh_part * tanh_part) * gelu_coeff * (
        1.0 + 3.0 * cubic_coeff * inputs * inputs
    )


RIGHT = [(i, (i + 1) % 4) for i in range(4)]
LEFT = [(i, (i + 3) % 4) for i in range(4)]
SWAP = [(0, 1), (1, 0)]
f32 = jnp.float32
bf16 = jnp.bfloat16


def tie(*values):
    return lax.optimization_barrier(values)


def shift(block, axis):
    return tie(lax.ppermute(block, axis, RIGHT), lax.ppermute(block, axis, LEFT))


def relay(left, right, axis):
    half = left.shape[0] // 2
    return tie(lax.ppermute(left[:half], axis, RIGHT), lax.ppermute(right[half:], axis, LEFT))


def place(blocks, axis, dim):
    me = lax.axis_index(axis)
    shape = blocks[0].shape
    out = jnp.zeros(shape[:dim] + (4,) + shape[dim:], blocks[0].dtype)
    for block, by in zip(blocks, (0, 3, 1, 2)):
        at = [0] * out.ndim
        at[dim] = lax.rem(me + by, 4)
        out = lax.dynamic_update_slice(out, jnp.expand_dims(block, dim), at)
    return out


def at(part, index, dim):
    return lax.dynamic_index_in_dim(part, index, dim, keepdims=False)


def add(one, other):
    return (one.astype(f32) + other.astype(f32)).astype(bf16)


def far_step(first, second, axis, dim):
    opposite = lax.rem(lax.axis_index(axis) + 2, 4)
    return tie(
        lax.ppermute(at(first, opposite, dim), axis, RIGHT), lax.ppermute(at(second, opposite, dim), axis, LEFT)
    )


def near_step(first, second, relayed, axis, dim):
    me = lax.axis_index(axis)
    right, left = lax.rem(me + 1, 4), lax.rem(me + 3, 4)
    to_right = jnp.stack([add(at(first, right, dim), relayed[0]), at(second, right, dim)])
    to_left = jnp.stack([at(first, left, dim), add(at(second, left, dim), relayed[1])])
    return tie(lax.ppermute(to_right, axis, RIGHT), lax.ppermute(to_left, axis, LEFT))


def home_step(first, second, near, axis, dim):
    me = lax.axis_index(axis)
    own = jnp.stack([at(first, me, dim), at(second, me, dim)])
    return own.astype(f32) + near[0].astype(f32) + near[1].astype(f32)


def collect(first, second, axis, dim):
    relayed = far_step(first, second, axis, dim)
    near = near_step(first, second, relayed, axis, dim)
    return home_step(first, second, near, axis, dim).astype(bf16)


def split_kernel(x_ref, rows_ref, out_ref):
    group, _, width = out_ref.shape
    for chip in range(group):
        out_ref[chip] = rows_ref[:, chip * width : (chip + 1) * width]


def split_quarter(hidden_in, x, chips):
    tok, ff_all = hidden_in.shape
    sub, ff, steps = tok // 4, ff_all // chips, 4
    return pl.pallas_call(
        split_kernel,
        grid_spec=pltpu.PrefetchScalarGridSpec(
            num_scalar_prefetch=1,
            grid=(steps,),
            in_specs=[pl.BlockSpec((sub, ff_all // steps), lambda step, x_ref: (x_ref[0], step))],
            out_specs=pl.BlockSpec((chips // steps, sub, ff), lambda step, x_ref: (step, 0, 0)),
        ),
        out_shape=jax.ShapeDtypeStruct((chips, sub, ff), hidden_in.dtype),
        name="split_quarter",
    )(x.astype(jnp.int32).reshape(1), hidden_in)


def body(hidden_in, down_weight, out_grad):
    tok, ff_all = hidden_in.shape
    ff_dev, cols = down_weight.shape
    ff = 2 * ff_dev
    sub = tok // 4
    x = lax.axis_index("x")
    core = lax.axis_index("core")
    plane = ("y", "z")

    mine = split_quarter(hidden_in, x, 16)
    mine, out_grad = tie(mine, out_grad)
    mine = lax.all_to_all(mine, plane, split_axis=0, concat_axis=0, tiled=True)
    mine = mine.reshape(4, 4, sub, ff)

    left_z, right_z = shift(out_grad, "z")
    far_z = jnp.concatenate(relay(left_z, right_z, "z"))
    line = place((out_grad, left_z, right_z, far_z), "z", 0)
    other_weight = lax.ppermute(down_weight, "core", SWAP)
    _, line, other_weight = tie(mine, line, other_weight)

    def activate(hidden):
        (act,) = tie(gelu_value(hidden.astype(f32)).astype(bf16))
        return act

    def forward(act):
        out = jnp.dot(act.reshape(16 * sub, ff), weight, preferred_element_type=f32)
        (out,) = tie(out.astype(bf16))
        return out.reshape(16, 1, sub, cols)

    def backward(grad):
        grad = grad.reshape(4 * tok, cols)
        out = lax.dot_general(grad, weight, (((1,), (1,)), ((), ())), preferred_element_type=f32)
        (out,) = tie(out.astype(bf16))
        return out.reshape(2, 2 * tok, ff)

    left, right = shift(mine, "x")
    left_y, right_y = shift(line, "y")
    weight = jnp.where(
        core == 0,
        jnp.concatenate([down_weight, other_weight]),
        jnp.concatenate([other_weight, down_weight]),
    )
    (weight,) = tie(weight)
    act_mine = activate(mine)
    part_mine = forward(act_mine)
    left, right, left_y, right_y, part_mine, act_mine, weight = tie(
        left, right, left_y, right_y, part_mine, act_mine, weight
    )

    far = relay(left, right, "x")
    far_y = relay(left_y, right_y, "y")
    act_left, act_right = activate(left), activate(right)
    terms_a = jnp.concatenate([part_mine, forward(act_left), forward(act_right)], axis=1)
    far, far_y, terms_a, act_left, act_right = lax.optimization_barrier((far, far_y, terms_a, act_left, act_right))

    terms_a = lax.all_to_all(terms_a, plane, split_axis=0, concat_axis=0, tiled=True)
    grad_all = place((line, left_y, right_y, jnp.concatenate(far_y)), "y", 0)
    quarter = lambda grad, by: backward(at(grad, lax.rem(x + by, 4), 0))
    opposite = quarter(grad_all, 2)
    opposite, grad_all, far = lax.optimization_barrier((opposite, grad_all, far))
    first, second = tie(lax.ppermute(opposite[0], "x", RIGHT), lax.ppermute(opposite[1], "x", LEFT))
    to_right, to_left = quarter(grad_all, 1), quarter(grad_all, 3)
    far = jnp.concatenate(far)
    act_far = activate(far)
    part_far = forward(act_far)
    first, second, to_right, to_left, part_far, act_far, grad_late = tie(
        first, second, to_right, to_left, part_far, act_far, grad_all
    )

    sum_right, sum_left = add(to_right[0], first), add(to_left[1], second)
    sum_right, sum_left = tie(lax.ppermute(sum_right, "x", RIGHT), lax.ppermute(sum_left, "x", LEFT))
    part_far = part_far.reshape(4, 4, 2, sub // 2, cols)
    part_far = (part_far[:, :, 0], part_far[:, :, 1])
    relayed = far_step(*part_far, "z", 1)
    home = quarter(grad_late, 0)
    sum_right, sum_left, relayed, to_right, to_left, part_far, grad_late, home = lax.optimization_barrier(
        (sum_right, sum_left, relayed, to_right[1], to_left[0], part_far, grad_late, home)
    )

    term_right, term_left = tie(lax.ppermute(to_right, "x", RIGHT), lax.ppermute(to_left, "x", LEFT))
    near = near_step(*part_far, relayed, "z", 1)

    rows = jnp.zeros((4, 4, sub, ff), bf16)
    active = jnp.zeros((4, 4, 4, sub, ff), bf16)
    chunks = (mine, left, right, far)
    acts = (act_mine, act_left, act_right, act_far)
    places = [lax.rem(x + by, 4) for by in (0, 3, 1, 2)]
    for chunk, act, j in zip(chunks, acts, places):
        rows = lax.dynamic_update_slice(rows, at(chunk, x, 0)[:, None], (0, j, 0, 0))
        active = lax.dynamic_update_slice(active, act[:, :, None], (0, 0, j, 0, 0))
    weight_sum = lax.dot_general(
        active.reshape(16 * tok, ff),
        grad_late.reshape(16 * tok, cols),
        (((0,), (0,)), ((), ())),
        preferred_element_type=f32,
    )
    (weight_sum,) = tie(weight_sum.astype(bf16))
    keep = lax.dynamic_slice(weight_sum, (ff_dev * core, 0), (ff_dev, cols))
    give = lax.dynamic_slice(weight_sum, (ff_dev * (1 - core), 0), (ff_dev, cols))
    take = lax.ppermute(give, "core", SWAP)
    weight_grad = ((keep.astype(f32) + take.astype(f32)) * float(32 * tok) ** (-0.5)).astype(bf16)
    term_right, term_left, near, part_far, weight_grad, rows = lax.optimization_barrier(
        (term_right, term_left, near, part_far, weight_grad, rows)
    )

    line_b = home_step(*part_far, near, "z", 1).astype(bf16)
    done_b = collect(line_b[0], line_b[1], "y", 0).reshape(sub, cols)

    def hidden_part(side):
        cut = lambda part: lax.dynamic_slice(part, (0, ff_dev * side), (part.shape[0], ff_dev)).astype(f32)
        slope = gelu_slope(cut(rows.reshape(4 * tok, ff)))
        from_left = jnp.concatenate([cut(sum_right), cut(term_right)])
        from_right = jnp.concatenate([cut(term_left), cut(sum_left)])
        summed = cut(home.reshape(4 * tok, ff)) + from_left + from_right
        return (summed * slope).astype(bf16).reshape(4, 1, tok, ff_dev)

    (give,) = tie(hidden_part(1 - core))
    take = lax.ppermute(give, "core", SWAP)
    hidden_grad = jnp.zeros((4, 2, tok, ff_dev), bf16)
    hidden_grad = lax.dynamic_update_slice(hidden_grad, hidden_part(core), (0, core, 0, 0))
    hidden_grad = lax.dynamic_update_slice(hidden_grad, take, (0, 1 - core, 0, 0))
    hidden_grad = hidden_grad.reshape(8 * tok, ff_dev)

    ffn_out = jnp.zeros((4, sub, cols), bf16)
    done_a = jnp.sum(terms_a.astype(f32), axis=0).astype(bf16)
    for done, j in zip((done_a[0], done_a[1], done_a[2], done_b), places):
        ffn_out = lax.dynamic_update_slice(ffn_out, done[None], (j, 0, 0))
    return (ffn_out.reshape(tok, cols), hidden_grad, weight_grad)


def solution(mesh):
    fine = Mesh(mesh.devices.reshape(4, 4, 2, 4), ("y", "z", "core", "x"))
    row = ("y", "z", "core")
    return jax.shard_map(
        body,
        mesh=fine,
        in_specs=(P(row, None), P(row, "x"), P(row, "x")),
        out_specs=(P(row, "x"), P("x", row), P(row, "x")),
        check_vma=False,
    )
```

```python
import functools

import jax
import jax.numpy as jnp
from jax import lax
from jax.experimental import pallas as pl
from jax.experimental.pallas import tpu as pltpu
from jax.sharding import Mesh, PartitionSpec as P

gelu_coeff = 0.7978845608
cubic_coeff = 0.044715


def gelu_value(inputs):
    inner = gelu_coeff * (inputs + cubic_coeff * inputs * inputs * inputs)
    return 0.5 * inputs * (1.0 + jnp.tanh(inner))


def gelu_slope(inputs):
    tanh_part = jnp.tanh(gelu_coeff * (inputs + cubic_coeff * inputs * inputs * inputs))
    return 0.5 * (1.0 + tanh_part) + 0.5 * inputs * (1.0 - tanh_part * tanh_part) * gelu_coeff * (
        1.0 + 3.0 * cubic_coeff * inputs * inputs
    )


RIGHT = [(i, (i + 1) % 4) for i in range(4)]
LEFT = [(i, (i + 3) % 4) for i in range(4)]
SWAP = [(0, 1), (1, 0)]
f32 = jnp.float32
bf16 = jnp.bfloat16


def tie(*values):
    return lax.optimization_barrier(values)


def shift(block, axis):
    return tie(lax.ppermute(block, axis, RIGHT), lax.ppermute(block, axis, LEFT))


def relay(left, right, axis):
    half = left.shape[0] // 2
    return tie(lax.ppermute(left[:half], axis, RIGHT), lax.ppermute(right[half:], axis, LEFT))


def place(blocks, axis, dim):
    me = lax.axis_index(axis)
    shape = blocks[0].shape
    out = jnp.zeros(shape[:dim] + (4,) + shape[dim:], blocks[0].dtype)
    for block, by in zip(blocks, (0, 3, 1, 2)):
        at = [0] * out.ndim
        at[dim] = lax.rem(me + by, 4)
        out = lax.dynamic_update_slice(out, jnp.expand_dims(block, dim), at)
    return out


def at(part, index, dim):
    return lax.dynamic_index_in_dim(part, index, dim, keepdims=False)


def add(one, other):
    return (one.astype(f32) + other.astype(f32)).astype(bf16)


def split_kernel(x_ref, rows_ref, out_ref):
    group, _, width = out_ref.shape
    for chip in range(group):
        out_ref[chip] = rows_ref[:, chip * width : (chip + 1) * width]


def split_quarter(hidden_in, x, chips):
    tok, ff_all = hidden_in.shape
    sub, ff, steps = tok // 4, ff_all // chips, 4
    return pl.pallas_call(
        split_kernel,
        grid_spec=pltpu.PrefetchScalarGridSpec(
            num_scalar_prefetch=1,
            grid=(steps,),
            in_specs=[pl.BlockSpec((sub, ff_all // steps), lambda step, x_ref: (x_ref[0], step))],
            out_specs=pl.BlockSpec((chips // steps, sub, ff), lambda step, x_ref: (step, 0, 0)),
        ),
        out_shape=jax.ShapeDtypeStruct((chips, sub, ff), hidden_in.dtype),
        name="split_quarter",
    )(x.astype(jnp.int32).reshape(1), hidden_in)


def weight_kernel(scale, at_ref, act_0, act_1, act_2, act_3, grad_0, grad_1, *rest):
    *other, out_ref, act, grad, total = rest
    pair = pl.program_id(0)
    rows = act_0.shape[0]

    @pl.when(pair == 0)
    def _():
        act[:rows] = act_0[...]
        act[rows:] = act_1[...]

    @pl.when(pair == 1)
    def _():
        act[:rows] = act_2[...]
        act[rows:] = act_3[...]

    grad[:rows] = grad_0[...].reshape(rows, grad.shape[1])
    grad[rows:] = grad_1[...].reshape(rows, grad.shape[1])
    term = lax.dot_general(act[...], grad[...], (((0,), (0,)), ((), ())), preferred_element_type=f32)

    @pl.when(pair == 0)
    def _():
        total[...] = term

    @pl.when(pair == 1)
    def _():
        done = total[...] + term
        for ref in other:
            done = (done + ref[...].astype(f32)) * scale
        out_ref[...] = done.astype(out_ref.dtype)


def weight_sum(acts, places, grad_all, side, other=(), scale=1.0):
    rows, ff = acts[0].shape
    chips, _, sub, cols = grad_all.shape
    whole = pl.BlockSpec((ff // 2, cols), lambda pair, at_ref: (0, 0))
    act_spec = pl.BlockSpec((rows, ff // 2), lambda pair, at_ref: (0, at_ref[4]))
    grad_specs = [
        pl.BlockSpec((chips, 1, sub, cols), lambda pair, at_ref, which=which: (0, at_ref[2 * pair + which], 0, 0))
        for which in (0, 1)
    ]
    return pl.pallas_call(
        functools.partial(weight_kernel, scale),
        grid_spec=pltpu.PrefetchScalarGridSpec(
            num_scalar_prefetch=1,
            grid=(2,),
            in_specs=[act_spec] * 4 + grad_specs + [whole] * len(other),
            out_specs=whole,
            scratch_shapes=[
                pltpu.VMEM((2 * rows, ff // 2), bf16),
                pltpu.VMEM((2 * rows, cols), bf16),
                pltpu.VMEM((ff // 2, cols), f32),
            ],
        ),
        out_shape=jax.ShapeDtypeStruct((ff // 2, cols), bf16),
        compiler_params=pltpu.CompilerParams(vmem_limit_bytes=48 * 2**20),
        cost_estimate=pl.CostEstimate(
            flops=4 * rows * ff * cols, bytes_accessed=4 * rows * (ff + 2 * cols) + 2 * ff * cols, transcendentals=0
        ),
        name="weight_sum",
    )(jnp.stack([*places, side]).astype(jnp.int32), *acts, grad_all, grad_all, *other)


def body(hidden_in, down_weight, out_grad):
    tok, ff_all = hidden_in.shape
    ff_dev, cols = down_weight.shape
    ff = 2 * ff_dev
    sub = tok // 4
    x = lax.axis_index("x")
    core = lax.axis_index("core")
    plane = ("y", "z")

    mine = split_quarter(hidden_in, x, 16)
    mine, out_grad = tie(mine, out_grad)
    mine = lax.all_to_all(mine, plane, split_axis=0, concat_axis=0, tiled=True)
    mine = mine.reshape(4, 4, sub, ff)

    left_z, right_z = shift(out_grad, "z")
    far_z = jnp.concatenate(relay(left_z, right_z, "z"))
    line = place((out_grad, left_z, right_z, far_z), "z", 0)
    other_weight = lax.ppermute(down_weight, "core", SWAP)
    _, line, other_weight = tie(mine, line, other_weight)

    def activate(hidden):
        (act,) = tie(gelu_value(hidden.astype(f32)).astype(bf16))
        return act

    def forward(act):
        out = jnp.dot(act.reshape(16 * sub, ff), weight, preferred_element_type=f32)
        (out,) = tie(out.astype(bf16))
        return out.reshape(16, 1, sub, cols)

    def backward(grad):
        grad = grad.reshape(4 * tok, cols)
        out = lax.dot_general(grad, weight, (((1,), (1,)), ((), ())), preferred_element_type=f32)
        (out,) = tie(out.astype(bf16))
        return out.reshape(2, 2 * tok, ff)

    def exchange(terms):
        return lax.all_to_all(terms, plane, split_axis=0, concat_axis=0, tiled=True)

    places = [lax.rem(x + by, 4) for by in (0, 3, 1, 2)]

    def with_rows(rows, chunk, j):
        return lax.dynamic_update_slice(rows, at(chunk, x, 0)[:, None], (0, j, 0, 0))

    left, right = shift(mine, "x")
    left_y, right_y = shift(line, "y")
    weight = jnp.where(
        core == 0,
        jnp.concatenate([down_weight, other_weight]),
        jnp.concatenate([other_weight, down_weight]),
    )
    (weight,) = tie(weight)
    act_mine = activate(mine)
    part_mine = forward(act_mine)
    rows = with_rows(jnp.zeros((4, 4, sub, ff), bf16), mine, places[0])
    left, right, left_y, right_y, part_mine, act_mine, weight, rows = tie(
        left, right, left_y, right_y, part_mine, act_mine, weight, rows
    )

    far = relay(left, right, "x")
    far_y = relay(left_y, right_y, "y")
    act_left, act_right = activate(left), activate(right)
    terms_a = jnp.concatenate([part_mine, forward(act_left)], axis=1)
    part_right = forward(act_right)
    rows = with_rows(with_rows(rows, left, places[1]), right, places[2])
    far, far_y, terms_a, part_right, act_left, act_right, rows = lax.optimization_barrier(
        (far, far_y, terms_a, part_right, act_left, act_right, rows)
    )

    terms_a = exchange(terms_a)
    grad_all = place((line, left_y, right_y, jnp.concatenate(far_y)), "y", 0)
    quarter = lambda grad, by: backward(at(grad, lax.rem(x + by, 4), 0))
    opposite = quarter(grad_all, 2)
    opposite, grad_all, far = lax.optimization_barrier((opposite, grad_all, far))
    first, second = tie(lax.ppermute(opposite[0], "x", RIGHT), lax.ppermute(opposite[1], "x", LEFT))
    to_right, to_left = quarter(grad_all, 1), quarter(grad_all, 3)
    far = jnp.concatenate(far)
    act_far = activate(far)
    terms_b = jnp.concatenate([part_right, forward(act_far)], axis=1)
    rows = with_rows(rows, far, places[3])
    first, second, to_right, to_left, terms_b, act_far, grad_late, rows = tie(
        first, second, to_right, to_left, terms_b, act_far, grad_all, rows
    )

    sum_right, sum_left = add(to_right[0], first), add(to_left[1], second)
    sum_right, sum_left = tie(lax.ppermute(sum_right, "x", RIGHT), lax.ppermute(sum_left, "x", LEFT))
    terms_b = exchange(terms_b)
    home = quarter(grad_late, 0)
    acts = [act.reshape(16 * sub, ff) for act in (act_mine, act_left, act_right, act_far)]
    terms_a, other_core = tie(terms_a, 1 - core)
    give_sum = weight_sum(acts, places, grad_late.reshape(16, 4, sub, cols), other_core)
    sum_right, sum_left, to_right, to_left, grad_late, home, give_sum = lax.optimization_barrier(
        (sum_right, sum_left, to_right[1], to_left[0], grad_late, home, give_sum)
    )

    term_right, term_left = tie(lax.ppermute(to_right, "x", RIGHT), lax.ppermute(to_left, "x", LEFT))
    take_sum = lax.ppermute(give_sum, "core", SWAP)
    weight_grad = weight_sum(
        acts, places, grad_late.reshape(16, 4, sub, cols), core, (take_sum,), float(32 * tok) ** (-0.5)
    )
    term_right, term_left, weight_grad = tie(term_right, term_left, weight_grad)

    slope = gelu_slope(rows.reshape(4 * tok, ff).astype(f32))
    from_left = jnp.concatenate([sum_right, term_right]).astype(f32)
    from_right = jnp.concatenate([term_left, sum_left]).astype(f32)
    summed = home.reshape(4 * tok, ff).astype(f32) + from_left + from_right
    (grad_here,) = tie((summed * slope).astype(bf16).reshape(4, 1, tok, ff))
    keep = lax.dynamic_slice(grad_here, (0, 0, 0, ff_dev * core), (4, 1, tok, ff_dev))
    give = lax.dynamic_slice(grad_here, (0, 0, 0, ff_dev * (1 - core)), (4, 1, tok, ff_dev))
    take = lax.ppermute(give, "core", SWAP)
    hidden_grad = jnp.zeros((4, 2, tok, ff_dev), bf16)
    hidden_grad = lax.dynamic_update_slice(hidden_grad, keep, (0, core, 0, 0))
    hidden_grad = lax.dynamic_update_slice(hidden_grad, take, (0, 1 - core, 0, 0))
    hidden_grad = hidden_grad.reshape(8 * tok, ff_dev)

    ffn_out = jnp.zeros((4, sub, cols), bf16)
    for terms, ends in ((terms_a, places[:2]), (terms_b, places[2:])):
        done = jnp.sum(terms.astype(f32), axis=0).astype(bf16)
        for which, j in enumerate(ends):
            ffn_out = lax.dynamic_update_slice(ffn_out, done[which][None], (j, 0, 0))
    return (ffn_out.reshape(tok, cols), hidden_grad, weight_grad)


def solution(mesh):
    fine = Mesh(mesh.devices.reshape(4, 4, 2, 4), ("y", "z", "core", "x"))
    row = ("y", "z", "core")
    return jax.shard_map(
        body,
        mesh=fine,
        in_specs=(P(row, None), P(row, "x"), P(row, "x")),
        out_specs=(P(row, "x"), P("x", row), P(row, "x")),
        check_vma=False,
    )
```

```python
import jax
import jax.numpy as jnp
from jax import lax
from jax.experimental import pallas as pl
from jax.experimental.pallas import tpu as pltpu
from jax.sharding import Mesh, PartitionSpec as P

gelu_coeff = 0.7978845608
cubic_coeff = 0.044715


def gelu_value(inputs):
    inner = gelu_coeff * (inputs + cubic_coeff * inputs * inputs * inputs)
    return 0.5 * inputs * (1.0 + jnp.tanh(inner))


def gelu_slope(inputs):
    tanh_part = jnp.tanh(gelu_coeff * (inputs + cubic_coeff * inputs * inputs * inputs))
    return 0.5 * (1.0 + tanh_part) + 0.5 * inputs * (1.0 - tanh_part * tanh_part) * gelu_coeff * (
        1.0 + 3.0 * cubic_coeff * inputs * inputs
    )


RIGHT = [(i, (i + 1) % 4) for i in range(4)]
LEFT = [(i, (i + 3) % 4) for i in range(4)]
SWAP = [(0, 1), (1, 0)]
f32 = jnp.float32
bf16 = jnp.bfloat16


def tie(*values):
    return lax.optimization_barrier(values)


def shift(block, axis):
    return tie(lax.ppermute(block, axis, RIGHT), lax.ppermute(block, axis, LEFT))


def relay(left, right, axis):
    half = left.shape[0] // 2
    return tie(lax.ppermute(left[:half], axis, RIGHT), lax.ppermute(right[half:], axis, LEFT))


def place(blocks, axis, dim):
    me = lax.axis_index(axis)
    shape = blocks[0].shape
    out = jnp.zeros(shape[:dim] + (4,) + shape[dim:], blocks[0].dtype)
    for block, by in zip(blocks, (0, 3, 1, 2)):
        at = [0] * out.ndim
        at[dim] = lax.rem(me + by, 4)
        out = lax.dynamic_update_slice(out, jnp.expand_dims(block, dim), at)
    return out


def at(part, index, dim):
    return lax.dynamic_index_in_dim(part, index, dim, keepdims=False)


def add(one, other):
    return (one.astype(f32) + other.astype(f32)).astype(bf16)


def split_kernel(x_ref, rows_ref, out_ref):
    group, _, width = out_ref.shape
    for chip in range(group):
        out_ref[chip] = rows_ref[:, chip * width : (chip + 1) * width]


def split_quarter(hidden_in, x, chips):
    tok, ff_all = hidden_in.shape
    sub, ff, steps = tok // 4, ff_all // chips, 4
    return pl.pallas_call(
        split_kernel,
        grid_spec=pltpu.PrefetchScalarGridSpec(
            num_scalar_prefetch=1,
            grid=(steps,),
            in_specs=[pl.BlockSpec((sub, ff_all // steps), lambda step, x_ref: (x_ref[0], step))],
            out_specs=pl.BlockSpec((chips // steps, sub, ff), lambda step, x_ref: (step, 0, 0)),
        ),
        out_shape=jax.ShapeDtypeStruct((chips, sub, ff), hidden_in.dtype),
        name="split_quarter",
    )(x.astype(jnp.int32).reshape(1), hidden_in)


def weight_kernel(at_ref, act_0, act_1, act_2, act_3, grad_0, grad_1, give_ref, keep_ref, act, grad, total):
    half, pair = pl.program_id(0), pl.program_id(1)
    rows = act_0.shape[0]

    @pl.when(pair == 0)
    def _():
        act[:rows] = act_0[...]
        act[rows:] = act_1[...]

    @pl.when(pair == 1)
    def _():
        act[:rows] = act_2[...]
        act[rows:] = act_3[...]

    grad[:rows] = grad_0[...].reshape(rows, grad.shape[1])
    grad[rows:] = grad_1[...].reshape(rows, grad.shape[1])
    term = lax.dot_general(act[...], grad[...], (((0,), (0,)), ((), ())), preferred_element_type=f32)

    @pl.when(pair == 0)
    def _():
        total[...] = term

    @pl.when((pair == 1) & (half == 0))
    def _():
        give_ref[...] = (total[...] + term).astype(give_ref.dtype)

    @pl.when((pair == 1) & (half == 1))
    def _():
        keep_ref[...] = (total[...] + term).astype(keep_ref.dtype)


def weight_sums(acts, places, grad_all, core):
    rows, ff = acts[0].shape
    chips, _, sub, cols = grad_all.shape
    act_spec = pl.BlockSpec((rows, ff // 2), lambda half, pair, at_ref: (0, lax.rem(at_ref[4] + half + 1, 2)))
    grad_specs = [
        pl.BlockSpec((chips, 1, sub, cols), lambda half, pair, at_ref, which=which: (0, at_ref[2 * pair + which], 0, 0))
        for which in (0, 1)
    ]
    return pl.pallas_call(
        weight_kernel,
        grid_spec=pltpu.PrefetchScalarGridSpec(
            num_scalar_prefetch=1,
            grid=(2, 2),
            in_specs=[act_spec] * 4 + grad_specs,
            out_specs=[pl.BlockSpec((ff // 2, cols), lambda half, pair, at_ref: (0, 0))] * 2,
            scratch_shapes=[
                pltpu.VMEM((2 * rows, ff // 2), bf16),
                pltpu.VMEM((2 * rows, cols), bf16),
                pltpu.VMEM((ff // 2, cols), f32),
            ],
        ),
        out_shape=[jax.ShapeDtypeStruct((ff // 2, cols), bf16)] * 2,
        compiler_params=pltpu.CompilerParams(vmem_limit_bytes=48 * 2**20),
        cost_estimate=pl.CostEstimate(
            flops=8 * rows * ff * cols, bytes_accessed=2 * (4 * rows * (ff + 2 * cols) + ff * cols), transcendentals=0
        ),
        name="weight_sums",
    )(jnp.stack([*places, core]).astype(jnp.int32), *acts, grad_all, grad_all)


def body(hidden_in, down_weight, out_grad):
    tok, ff_all = hidden_in.shape
    ff_dev, cols = down_weight.shape
    ff = 2 * ff_dev
    sub = tok // 4
    x = lax.axis_index("x")
    core = lax.axis_index("core")
    plane = ("y", "z")

    mine = split_quarter(hidden_in, x, 16)
    mine, out_grad = tie(mine, out_grad)
    mine = lax.all_to_all(mine, plane, split_axis=0, concat_axis=0, tiled=True)
    mine = mine.reshape(4, 4, sub, ff)

    left_z, right_z = shift(out_grad, "z")
    far_z = jnp.concatenate(relay(left_z, right_z, "z"))
    line = place((out_grad, left_z, right_z, far_z), "z", 0)
    other_weight = lax.ppermute(down_weight, "core", SWAP)
    _, line, other_weight = tie(mine, line, other_weight)

    def activate(hidden):
        (act,) = tie(gelu_value(hidden.astype(f32)).astype(bf16))
        return act

    def forward(act):
        out = jnp.dot(act.reshape(16 * sub, ff), weight, preferred_element_type=f32)
        (out,) = tie(out.astype(bf16))
        return out.reshape(16, 1, sub, cols)

    def backward(grad):
        grad = grad.reshape(4 * tok, cols)
        out = lax.dot_general(grad, weight, (((1,), (1,)), ((), ())), preferred_element_type=f32)
        (out,) = tie(out.astype(bf16))
        return out.reshape(2, 2 * tok, ff)

    def exchange(terms):
        return lax.all_to_all(terms, plane, split_axis=0, concat_axis=0, tiled=True)

    places = [lax.rem(x + by, 4) for by in (0, 3, 1, 2)]

    def with_rows(rows, chunk, j):
        return lax.dynamic_update_slice(rows, at(chunk, x, 0)[:, None], (0, j, 0, 0))

    left, right = shift(mine, "x")
    left_y, right_y = shift(line, "y")
    weight = jnp.where(
        core == 0,
        jnp.concatenate([down_weight, other_weight]),
        jnp.concatenate([other_weight, down_weight]),
    )
    (weight,) = tie(weight)
    act_mine = activate(mine)
    part_mine = forward(act_mine)
    rows = with_rows(jnp.zeros((4, 4, sub, ff), bf16), mine, places[0])
    left, right, left_y, right_y, part_mine, act_mine, weight, rows = tie(
        left, right, left_y, right_y, part_mine, act_mine, weight, rows
    )

    far = relay(left, right, "x")
    far_y = relay(left_y, right_y, "y")
    act_left, act_right = activate(left), activate(right)
    terms_a = jnp.concatenate([part_mine, forward(act_left)], axis=1)
    part_right = forward(act_right)
    rows = with_rows(with_rows(rows, left, places[1]), right, places[2])
    far, far_y, terms_a, part_right, act_left, act_right, rows = lax.optimization_barrier(
        (far, far_y, terms_a, part_right, act_left, act_right, rows)
    )

    terms_a = exchange(terms_a)
    grad_all = place((line, left_y, right_y, jnp.concatenate(far_y)), "y", 0)
    quarter = lambda grad, by: backward(at(grad, lax.rem(x + by, 4), 0))
    opposite = quarter(grad_all, 2)
    opposite, grad_all, far = lax.optimization_barrier((opposite, grad_all, far))
    first, second = tie(lax.ppermute(opposite[0], "x", RIGHT), lax.ppermute(opposite[1], "x", LEFT))
    to_right, to_left = quarter(grad_all, 1), quarter(grad_all, 3)
    far = jnp.concatenate(far)
    act_far = activate(far)
    terms_b = jnp.concatenate([part_right, forward(act_far)], axis=1)
    rows = with_rows(rows, far, places[3])
    first, second, to_right, to_left, terms_b, act_far, grad_late, rows = tie(
        first, second, to_right, to_left, terms_b, act_far, grad_all, rows
    )

    sum_right, sum_left = add(to_right[0], first), add(to_left[1], second)
    sum_right, sum_left = tie(lax.ppermute(sum_right, "x", RIGHT), lax.ppermute(sum_left, "x", LEFT))
    terms_b = exchange(terms_b)
    terms_a, me = tie(terms_a, x)
    home = backward(at(grad_late, me, 0))
    sum_right, sum_left, to_right, to_left, grad_late, home = lax.optimization_barrier(
        (sum_right, sum_left, to_right[1], to_left[0], grad_late, home)
    )

    term_right, term_left = tie(lax.ppermute(to_right, "x", RIGHT), lax.ppermute(to_left, "x", LEFT))
    acts = [act.reshape(16 * sub, ff) for act in (act_mine, act_left, act_right, act_far)]
    give_sum, keep_sum = weight_sums(acts, places, grad_late.reshape(16, 4, sub, cols), core)
    term_right, term_left, give_sum, keep_sum = tie(term_right, term_left, give_sum, keep_sum)

    take_sum = lax.ppermute(give_sum, "core", SWAP)
    weight_grad = (keep_sum.astype(f32) + take_sum.astype(f32)) * float(32 * tok) ** (-0.5)
    weight_grad = weight_grad.astype(bf16)

    slope = gelu_slope(rows.reshape(4 * tok, ff).astype(f32))
    from_left = jnp.concatenate([sum_right, term_right]).astype(f32)
    from_right = jnp.concatenate([term_left, sum_left]).astype(f32)
    summed = home.reshape(4 * tok, ff).astype(f32) + from_left + from_right
    grad_here, terms_b = tie((summed * slope).astype(bf16).reshape(4, 1, tok, ff), terms_b)
    keep = lax.dynamic_slice(grad_here, (0, 0, 0, ff_dev * core), (4, 1, tok, ff_dev))
    give = lax.dynamic_slice(grad_here, (0, 0, 0, ff_dev * (1 - core)), (4, 1, tok, ff_dev))
    take = lax.ppermute(give, "core", SWAP)
    hidden_grad = jnp.zeros((4, 2, tok, ff_dev), bf16)
    hidden_grad = lax.dynamic_update_slice(hidden_grad, keep, (0, core, 0, 0))
    hidden_grad = lax.dynamic_update_slice(hidden_grad, take, (0, 1 - core, 0, 0))
    hidden_grad = hidden_grad.reshape(8 * tok, ff_dev)

    ffn_out = jnp.zeros((4, sub, cols), bf16)
    for terms, ends in ((terms_a, places[:2]), (terms_b, places[2:])):
        done = jnp.sum(terms.astype(f32), axis=0).astype(bf16)
        for which, j in enumerate(ends):
            ffn_out = lax.dynamic_update_slice(ffn_out, done[which][None], (j, 0, 0))
    return (ffn_out.reshape(tok, cols), hidden_grad, weight_grad)


def solution(mesh):
    fine = Mesh(mesh.devices.reshape(4, 4, 2, 4), ("y", "z", "core", "x"))
    row = ("y", "z", "core")
    return jax.shard_map(
        body,
        mesh=fine,
        in_specs=(P(row, None), P(row, "x"), P(row, "x")),
        out_specs=(P(row, "x"), P("x", row), P(row, "x")),
        check_vma=False,
    )
```

```python
import jax
import jax.numpy as jnp
from jax import lax
from jax.experimental import pallas as pl
from jax.experimental.pallas import tpu as pltpu
from jax.sharding import Mesh, PartitionSpec as P

gelu_coeff = 0.7978845608
cubic_coeff = 0.044715


def gelu_value(inputs):
    inner = gelu_coeff * (inputs + cubic_coeff * inputs * inputs * inputs)
    return 0.5 * inputs * (1.0 + jnp.tanh(inner))


def gelu_slope(inputs):
    tanh_part = jnp.tanh(gelu_coeff * (inputs + cubic_coeff * inputs * inputs * inputs))
    return 0.5 * (1.0 + tanh_part) + 0.5 * inputs * (1.0 - tanh_part * tanh_part) * gelu_coeff * (
        1.0 + 3.0 * cubic_coeff * inputs * inputs
    )


RIGHT = [(i, (i + 1) % 4) for i in range(4)]
LEFT = [(i, (i + 3) % 4) for i in range(4)]
SWAP = [(0, 1), (1, 0)]
f32 = jnp.float32
bf16 = jnp.bfloat16


def tie(*values):
    return lax.optimization_barrier(values)


def shift(block, axis):
    return tie(lax.ppermute(block, axis, RIGHT), lax.ppermute(block, axis, LEFT))


def relay(left, right, axis):
    half = left.shape[0] // 2
    return tie(lax.ppermute(left[:half], axis, RIGHT), lax.ppermute(right[half:], axis, LEFT))


def place(blocks, axis, dim):
    me = lax.axis_index(axis)
    shape = blocks[0].shape
    out = jnp.zeros(shape[:dim] + (4,) + shape[dim:], blocks[0].dtype)
    for block, by in zip(blocks, (0, 3, 1, 2)):
        at = [0] * out.ndim
        at[dim] = lax.rem(me + by, 4)
        out = lax.dynamic_update_slice(out, jnp.expand_dims(block, dim), at)
    return out


def at(part, index, dim):
    return lax.dynamic_index_in_dim(part, index, dim, keepdims=False)


def add(one, other):
    return (one.astype(f32) + other.astype(f32)).astype(bf16)


def split_kernel(x_ref, rows_ref, out_ref):
    group, _, width = out_ref.shape
    for chip in range(group):
        out_ref[chip] = rows_ref[:, chip * width : (chip + 1) * width]


def split_quarter(hidden_in, x, chips):
    tok, ff_all = hidden_in.shape
    sub, ff, steps = tok // 4, ff_all // chips, 4
    return pl.pallas_call(
        split_kernel,
        grid_spec=pltpu.PrefetchScalarGridSpec(
            num_scalar_prefetch=1,
            grid=(steps,),
            in_specs=[pl.BlockSpec((sub, ff_all // steps), lambda step, x_ref: (x_ref[0], step))],
            out_specs=pl.BlockSpec((chips // steps, sub, ff), lambda step, x_ref: (step, 0, 0)),
        ),
        out_shape=jax.ShapeDtypeStruct((chips, sub, ff), hidden_in.dtype),
        name="split_quarter",
    )(x.astype(jnp.int32).reshape(1), hidden_in)


def weight_kernel(at_ref, act_0, act_1, act_2, act_3, grad_0, grad_1, give_ref, keep_ref, act, grad, total):
    half, pair = pl.program_id(0), pl.program_id(1)
    rows = act_0.shape[0]

    @pl.when(pair == 0)
    def _():
        act[:rows] = act_0[...]
        act[rows:] = act_1[...]

    @pl.when(pair == 1)
    def _():
        act[:rows] = act_2[...]
        act[rows:] = act_3[...]

    grad[:rows] = grad_0[...].reshape(rows, grad.shape[1])
    grad[rows:] = grad_1[...].reshape(rows, grad.shape[1])
    term = lax.dot_general(act[...], grad[...], (((0,), (0,)), ((), ())), preferred_element_type=f32)

    @pl.when(pair == 0)
    def _():
        total[...] = term

    @pl.when((pair == 1) & (half == 0))
    def _():
        give_ref[...] = (total[...] + term).astype(give_ref.dtype)

    @pl.when((pair == 1) & (half == 1))
    def _():
        keep_ref[...] = (total[...] + term).astype(keep_ref.dtype)


def weight_sums(acts, places, grad_all, core):
    rows, ff = acts[0].shape
    chips, _, sub, cols = grad_all.shape
    act_spec = pl.BlockSpec((rows, ff // 2), lambda half, pair, at_ref: (0, lax.rem(at_ref[4] + half + 1, 2)))
    grad_specs = [
        pl.BlockSpec((chips, 1, sub, cols), lambda half, pair, at_ref, which=which: (0, at_ref[2 * pair + which], 0, 0))
        for which in (0, 1)
    ]
    return pl.pallas_call(
        weight_kernel,
        grid_spec=pltpu.PrefetchScalarGridSpec(
            num_scalar_prefetch=1,
            grid=(2, 2),
            in_specs=[act_spec] * 4 + grad_specs,
            out_specs=[pl.BlockSpec((ff // 2, cols), lambda half, pair, at_ref: (0, 0))] * 2,
            scratch_shapes=[
                pltpu.VMEM((2 * rows, ff // 2), bf16),
                pltpu.VMEM((2 * rows, cols), bf16),
                pltpu.VMEM((ff // 2, cols), f32),
            ],
        ),
        out_shape=[jax.ShapeDtypeStruct((ff // 2, cols), bf16)] * 2,
        compiler_params=pltpu.CompilerParams(vmem_limit_bytes=48 * 2**20),
        cost_estimate=pl.CostEstimate(
            flops=8 * rows * ff * cols, bytes_accessed=2 * (4 * rows * (ff + 2 * cols) + ff * cols), transcendentals=0
        ),
        name="weight_sums",
    )(jnp.stack([*places, core]).astype(jnp.int32), *acts, grad_all, grad_all)


def body(hidden_in, down_weight, out_grad):
    tok, ff_all = hidden_in.shape
    ff_dev, cols = down_weight.shape
    ff = 2 * ff_dev
    sub = tok // 4
    x = lax.axis_index("x")
    core = lax.axis_index("core")
    plane = ("y", "z")

    mine = split_quarter(hidden_in, x, 16)
    mine, out_grad = tie(mine, out_grad)
    mine = lax.all_to_all(mine, plane, split_axis=0, concat_axis=0, tiled=True)
    mine = mine.reshape(4, 4, sub, ff)

    left_z, right_z = shift(out_grad, "z")
    far_z = jnp.concatenate(relay(left_z, right_z, "z"))
    line = place((out_grad, left_z, right_z, far_z), "z", 0)
    other_weight = lax.ppermute(down_weight, "core", SWAP)
    _, line, other_weight = tie(mine, line, other_weight)

    def activate(hidden):
        (act,) = tie(gelu_value(hidden.astype(f32)).astype(bf16))
        return act

    def forward(act):
        out = jnp.dot(act.reshape(16 * sub, ff), weight, preferred_element_type=f32)
        (out,) = tie(out.astype(bf16))
        return out.reshape(16, 1, sub, cols)

    def backward(grad):
        grad = grad.reshape(4 * tok, cols)
        out = lax.dot_general(grad, weight, (((1,), (1,)), ((), ())), preferred_element_type=f32)
        (out,) = tie(out.astype(bf16))
        return out.reshape(2, 2 * tok, ff)

    def exchange(terms):
        return lax.all_to_all(terms, plane, split_axis=0, concat_axis=0, tiled=True)

    places = [lax.rem(x + by, 4) for by in (0, 3, 1, 2)]

    def with_rows(rows, chunk, j):
        return lax.dynamic_update_slice(rows, at(chunk, x, 0)[:, None], (0, j, 0, 0))

    left, right = shift(mine, "x")
    left_y, right_y = shift(line, "y")
    weight = jnp.where(
        core == 0,
        jnp.concatenate([down_weight, other_weight]),
        jnp.concatenate([other_weight, down_weight]),
    )
    (weight,) = tie(weight)
    act_mine = activate(mine)
    part_mine = forward(act_mine)
    rows = with_rows(jnp.zeros((4, 4, sub, ff), bf16), mine, places[0])
    left, right, left_y, right_y, part_mine, act_mine, weight, rows = tie(
        left, right, left_y, right_y, part_mine, act_mine, weight, rows
    )

    far = relay(left, right, "x")
    far_y = relay(left_y, right_y, "y")
    act_left, act_right = activate(left), activate(right)
    terms_a = jnp.concatenate([part_mine, forward(act_left)], axis=1)
    part_right = forward(act_right)
    rows = with_rows(with_rows(rows, left, places[1]), right, places[2])
    far, far_y, terms_a, part_right, act_left, act_right, rows = lax.optimization_barrier(
        (far, far_y, terms_a, part_right, act_left, act_right, rows)
    )

    terms_a = exchange(terms_a)
    grad_all = place((line, left_y, right_y, jnp.concatenate(far_y)), "y", 0)
    quarter = lambda grad, by: backward(at(grad, lax.rem(x + by, 4), 0))
    opposite = quarter(grad_all, 2)
    opposite, grad_all, far = lax.optimization_barrier((opposite, grad_all, far))
    first, second = tie(lax.ppermute(opposite[0], "x", RIGHT), lax.ppermute(opposite[1], "x", LEFT))
    to_right, to_left = quarter(grad_all, 1), quarter(grad_all, 3)
    far = jnp.concatenate(far)
    act_far = activate(far)
    terms_b = jnp.concatenate([part_right, forward(act_far)], axis=1)
    rows = with_rows(rows, far, places[3])
    first, second, to_right, to_left, terms_b, act_far, grad_late, rows = tie(
        first, second, to_right, to_left, terms_b, act_far, grad_all, rows
    )

    sum_right, sum_left = add(to_right[0], first), add(to_left[1], second)
    sum_right, sum_left = tie(lax.ppermute(sum_right, "x", RIGHT), lax.ppermute(sum_left, "x", LEFT))
    terms_b = exchange(terms_b)
    home = quarter(grad_late, 0)
    sum_right, sum_left, to_right, to_left, grad_late, home, terms_a = lax.optimization_barrier(
        (sum_right, sum_left, to_right[1], to_left[0], grad_late, home, terms_a)
    )

    term_right, term_left = tie(lax.ppermute(to_right, "x", RIGHT), lax.ppermute(to_left, "x", LEFT))
    acts = [act.reshape(16 * sub, ff) for act in (act_mine, act_left, act_right, act_far)]
    give_sum, keep_sum = weight_sums(acts, places, grad_late.reshape(16, 4, sub, cols), core)
    term_right, term_left, give_sum, keep_sum = tie(term_right, term_left, give_sum, keep_sum)

    take_sum = lax.ppermute(give_sum, "core", SWAP)
    weight_grad = (keep_sum.astype(f32) + take_sum.astype(f32)) * float(32 * tok) ** (-0.5)
    weight_grad = weight_grad.astype(bf16)

    slope = gelu_slope(rows.reshape(4 * tok, ff).astype(f32))
    from_left = jnp.concatenate([sum_right, term_right]).astype(f32)
    from_right = jnp.concatenate([term_left, sum_left]).astype(f32)
    summed = home.reshape(4 * tok, ff).astype(f32) + from_left + from_right
    grad_here, terms_b = tie((summed * slope).astype(bf16).reshape(4, 1, tok, ff), terms_b)
    keep = lax.dynamic_slice(grad_here, (0, 0, 0, ff_dev * core), (4, 1, tok, ff_dev))
    give = lax.dynamic_slice(grad_here, (0, 0, 0, ff_dev * (1 - core)), (4, 1, tok, ff_dev))
    take = lax.ppermute(give, "core", SWAP)
    hidden_grad = jnp.zeros((4, 2, tok, ff_dev), bf16)
    hidden_grad = lax.dynamic_update_slice(hidden_grad, keep, (0, core, 0, 0))
    hidden_grad = lax.dynamic_update_slice(hidden_grad, take, (0, 1 - core, 0, 0))
    hidden_grad = hidden_grad.reshape(8 * tok, ff_dev)

    ffn_out = jnp.zeros((4, sub, cols), bf16)
    for terms, ends in ((terms_a, places[:2]), (terms_b, places[2:])):
        done = jnp.sum(terms.astype(f32), axis=0).astype(bf16)
        for which, j in enumerate(ends):
            ffn_out = lax.dynamic_update_slice(ffn_out, done[which][None], (j, 0, 0))
    return (ffn_out.reshape(tok, cols), hidden_grad, weight_grad)


def solution(mesh):
    fine = Mesh(mesh.devices.reshape(4, 4, 2, 4), ("y", "z", "core", "x"))
    row = ("y", "z", "core")
    return jax.shard_map(
        body,
        mesh=fine,
        in_specs=(P(row, None), P(row, "x"), P(row, "x")),
        out_specs=(P(row, "x"), P("x", row), P(row, "x")),
        check_vma=False,
    )
```

```python
import jax
import jax.numpy as jnp
from jax import lax
from jax.experimental import pallas as pl
from jax.experimental.pallas import tpu as pltpu
from jax.sharding import Mesh, PartitionSpec as P

gelu_coeff = 0.7978845608
cubic_coeff = 0.044715


def gelu_value(inputs):
    inner = gelu_coeff * (inputs + cubic_coeff * inputs * inputs * inputs)
    return 0.5 * inputs * (1.0 + jnp.tanh(inner))


def gelu_slope(inputs):
    tanh_part = jnp.tanh(gelu_coeff * (inputs + cubic_coeff * inputs * inputs * inputs))
    return 0.5 * (1.0 + tanh_part) + 0.5 * inputs * (1.0 - tanh_part * tanh_part) * gelu_coeff * (
        1.0 + 3.0 * cubic_coeff * inputs * inputs
    )


RIGHT = [(i, (i + 1) % 4) for i in range(4)]
LEFT = [(i, (i + 3) % 4) for i in range(4)]
SWAP = [(0, 1), (1, 0)]
f32 = jnp.float32
bf16 = jnp.bfloat16


def tie(*values):
    return lax.optimization_barrier(values)


def shift(block, axis):
    return tie(lax.ppermute(block, axis, RIGHT), lax.ppermute(block, axis, LEFT))


def relay(left, right, axis):
    half = left.shape[0] // 2
    return tie(lax.ppermute(left[:half], axis, RIGHT), lax.ppermute(right[half:], axis, LEFT))


def place(blocks, axis, dim):
    me = lax.axis_index(axis)
    shape = blocks[0].shape
    out = jnp.zeros(shape[:dim] + (4,) + shape[dim:], blocks[0].dtype)
    for block, by in zip(blocks, (0, 3, 1, 2)):
        at = [0] * out.ndim
        at[dim] = lax.rem(me + by, 4)
        out = lax.dynamic_update_slice(out, jnp.expand_dims(block, dim), at)
    return out


def at(part, index, dim):
    return lax.dynamic_index_in_dim(part, index, dim, keepdims=False)


def add(one, other):
    return (one.astype(f32) + other.astype(f32)).astype(bf16)


def split_kernel(x_ref, rows_ref, out_ref):
    group, _, width = out_ref.shape
    for chip in range(group):
        out_ref[chip] = rows_ref[:, chip * width : (chip + 1) * width]


def split_quarter(hidden_in, x, chips):
    tok, ff_all = hidden_in.shape
    sub, ff, steps = tok // 4, ff_all // chips, 4
    return pl.pallas_call(
        split_kernel,
        grid_spec=pltpu.PrefetchScalarGridSpec(
            num_scalar_prefetch=1,
            grid=(steps,),
            in_specs=[pl.BlockSpec((sub, ff_all // steps), lambda step, x_ref: (x_ref[0], step))],
            out_specs=pl.BlockSpec((chips // steps, sub, ff), lambda step, x_ref: (step, 0, 0)),
        ),
        out_shape=jax.ShapeDtypeStruct((chips, sub, ff), hidden_in.dtype),
        name="split_quarter",
    )(x.astype(jnp.int32).reshape(1), hidden_in)


def weight_kernel(at_ref, act_0, act_1, act_2, act_3, grad_0, grad_1, give_ref, keep_ref, act, grad, total):
    half, pair = pl.program_id(0), pl.program_id(1)
    rows = act_0.shape[0]

    @pl.when(pair == 0)
    def _():
        act[:rows] = act_0[...]
        act[rows:] = act_1[...]

    @pl.when(pair == 1)
    def _():
        act[:rows] = act_2[...]
        act[rows:] = act_3[...]

    grad[:rows] = grad_0[...].reshape(rows, grad.shape[1])
    grad[rows:] = grad_1[...].reshape(rows, grad.shape[1])
    term = lax.dot_general(act[...], grad[...], (((0,), (0,)), ((), ())), preferred_element_type=f32)

    @pl.when(pair == 0)
    def _():
        total[...] = term

    @pl.when((pair == 1) & (half == 0))
    def _():
        give_ref[...] = (total[...] + term).astype(give_ref.dtype)

    @pl.when((pair == 1) & (half == 1))
    def _():
        keep_ref[...] = (total[...] + term).astype(keep_ref.dtype)


def weight_sums(acts, places, grad_all, core):
    rows, ff = acts[0].shape
    chips, _, sub, cols = grad_all.shape
    act_spec = pl.BlockSpec((rows, ff // 2), lambda half, pair, at_ref: (0, lax.rem(at_ref[4] + half + 1, 2)))
    grad_specs = [
        pl.BlockSpec((chips, 1, sub, cols), lambda half, pair, at_ref, which=which: (0, at_ref[2 * pair + which], 0, 0))
        for which in (0, 1)
    ]
    return pl.pallas_call(
        weight_kernel,
        grid_spec=pltpu.PrefetchScalarGridSpec(
            num_scalar_prefetch=1,
            grid=(2, 2),
            in_specs=[act_spec] * 4 + grad_specs,
            out_specs=[pl.BlockSpec((ff // 2, cols), lambda half, pair, at_ref: (0, 0))] * 2,
            scratch_shapes=[
                pltpu.VMEM((2 * rows, ff // 2), bf16),
                pltpu.VMEM((2 * rows, cols), bf16),
                pltpu.VMEM((ff // 2, cols), f32),
            ],
        ),
        out_shape=[jax.ShapeDtypeStruct((ff // 2, cols), bf16)] * 2,
        compiler_params=pltpu.CompilerParams(vmem_limit_bytes=48 * 2**20),
        cost_estimate=pl.CostEstimate(
            flops=8 * rows * ff * cols, bytes_accessed=2 * (4 * rows * (ff + 2 * cols) + ff * cols), transcendentals=0
        ),
        name="weight_sums",
    )(jnp.stack([*places, core]).astype(jnp.int32), *acts, grad_all, grad_all)


def body(hidden_in, down_weight, out_grad):
    tok, ff_all = hidden_in.shape
    ff_dev, cols = down_weight.shape
    ff = 2 * ff_dev
    sub = tok // 4
    x = lax.axis_index("x")
    core = lax.axis_index("core")
    plane = ("y", "z")

    mine = split_quarter(hidden_in, x, 16)
    mine, out_grad = tie(mine, out_grad)
    mine = lax.all_to_all(mine, plane, split_axis=0, concat_axis=0, tiled=True)
    mine = mine.reshape(4, 4, sub, ff)

    left_z, right_z = shift(out_grad, "z")
    far_z = jnp.concatenate(relay(left_z, right_z, "z"))
    line = place((out_grad, left_z, right_z, far_z), "z", 0)
    other_weight = lax.ppermute(down_weight, "core", SWAP)
    _, line, other_weight = tie(mine, line, other_weight)

    def activate(hidden):
        (act,) = tie(gelu_value(hidden.astype(f32)).astype(bf16))
        return act

    def forward(act):
        out = jnp.dot(act.reshape(16 * sub, ff), weight, preferred_element_type=f32)
        (out,) = tie(out.astype(bf16))
        return out.reshape(16, 1, sub, cols)

    def backward(grad):
        grad = grad.reshape(4 * tok, cols)
        out = lax.dot_general(grad, weight, (((1,), (1,)), ((), ())), preferred_element_type=f32)
        (out,) = tie(out.astype(bf16))
        return out.reshape(2, 2 * tok, ff)

    def exchange(terms):
        return lax.all_to_all(terms, plane, split_axis=0, concat_axis=0, tiled=True)

    places = [lax.rem(x + by, 4) for by in (0, 3, 1, 2)]

    def with_rows(rows, chunk, j):
        return lax.dynamic_update_slice(rows, at(chunk, x, 0)[:, None], (0, j, 0, 0))

    left, right = shift(mine, "x")
    left_y, right_y = shift(line, "y")
    weight = jnp.where(
        core == 0,
        jnp.concatenate([down_weight, other_weight]),
        jnp.concatenate([other_weight, down_weight]),
    )
    (weight,) = tie(weight)
    act_mine = activate(mine)
    part_mine = forward(act_mine)
    rows = with_rows(jnp.zeros((4, 4, sub, ff), bf16), mine, places[0])
    left, right, left_y, right_y, part_mine, act_mine, weight, rows = tie(
        left, right, left_y, right_y, part_mine, act_mine, weight, rows
    )

    far = relay(left, right, "x")
    far_y = relay(left_y, right_y, "y")
    act_left, act_right = activate(left), activate(right)
    terms_a = jnp.concatenate([part_mine, forward(act_left)], axis=1)
    part_right = forward(act_right)
    rows = with_rows(with_rows(rows, left, places[1]), right, places[2])
    far, far_y, terms_a, part_right, act_left, act_right, rows = lax.optimization_barrier(
        (far, far_y, terms_a, part_right, act_left, act_right, rows)
    )

    terms_a = exchange(terms_a)
    grad_all = place((line, left_y, right_y, jnp.concatenate(far_y)), "y", 0)
    quarter = lambda grad, by: backward(at(grad, lax.rem(x + by, 4), 0))
    opposite = quarter(grad_all, 2)
    opposite, grad_all, far = lax.optimization_barrier((opposite, grad_all, far))
    first, second = tie(lax.ppermute(opposite[0], "x", RIGHT), lax.ppermute(opposite[1], "x", LEFT))
    to_right, to_left = quarter(grad_all, 1), quarter(grad_all, 3)
    far = jnp.concatenate(far)
    act_far = activate(far)
    terms_b = jnp.concatenate([part_right, forward(act_far)], axis=1)
    rows = with_rows(rows, far, places[3])
    first, second, to_right, to_left, terms_b, act_far, grad_late, rows = tie(
        first, second, to_right, to_left, terms_b, act_far, grad_all, rows
    )

    sum_right, sum_left = add(to_right[0], first), add(to_left[1], second)
    sum_right, sum_left = tie(lax.ppermute(sum_right, "x", RIGHT), lax.ppermute(sum_left, "x", LEFT))
    terms_b = exchange(terms_b)
    terms_a, me = tie(terms_a, x)
    home = backward(at(grad_late, me, 0))
    sum_right, sum_left, to_right, to_left, grad_late, home = lax.optimization_barrier(
        (sum_right, sum_left, to_right[1], to_left[0], grad_late, home)
    )

    term_right, term_left = tie(lax.ppermute(to_right, "x", RIGHT), lax.ppermute(to_left, "x", LEFT))
    acts = [act.reshape(16 * sub, ff) for act in (act_mine, act_left, act_right, act_far)]
    give_sum, keep_sum = weight_sums(acts, places, grad_late.reshape(16, 4, sub, cols), core)
    term_right, term_left, give_sum, keep_sum = tie(term_right, term_left, give_sum, keep_sum)

    take_sum = lax.ppermute(give_sum, "core", SWAP)
    weight_grad = (keep_sum.astype(f32) + take_sum.astype(f32)) * float(32 * tok) ** (-0.5)
    weight_grad = weight_grad.astype(bf16)

    slope = gelu_slope(rows.reshape(4 * tok, ff).astype(f32))
    sides = ((sum_right, term_left), (term_right, sum_left))
    parts = []
    for piece, (one, other) in enumerate(sides):
        summed = home[piece].astype(f32) + one.astype(f32) + other.astype(f32)
        parts.append((summed * slope[2 * tok * piece : 2 * tok * (piece + 1)]).astype(bf16).reshape(2, 1, tok, ff))
    *parts, terms_b = tie(*parts, terms_b)
    hidden_grad = jnp.zeros((4, 2, tok, ff_dev), bf16)
    for piece, part in enumerate(parts):
        keep = lax.dynamic_slice(part, (0, 0, 0, ff_dev * core), (2, 1, tok, ff_dev))
        give = lax.dynamic_slice(part, (0, 0, 0, ff_dev * (1 - core)), (2, 1, tok, ff_dev))
        take = lax.ppermute(give, "core", SWAP)
        hidden_grad = lax.dynamic_update_slice(hidden_grad, keep, (2 * piece, core, 0, 0))
        hidden_grad = lax.dynamic_update_slice(hidden_grad, take, (2 * piece, 1 - core, 0, 0))
    hidden_grad = hidden_grad.reshape(8 * tok, ff_dev)

    ffn_out = jnp.zeros((4, sub, cols), bf16)
    for terms, ends in ((terms_a, places[:2]), (terms_b, places[2:])):
        done = jnp.sum(terms.astype(f32), axis=0).astype(bf16)
        for which, j in enumerate(ends):
            ffn_out = lax.dynamic_update_slice(ffn_out, done[which][None], (j, 0, 0))
    return (ffn_out.reshape(tok, cols), hidden_grad, weight_grad)


def solution(mesh):
    fine = Mesh(mesh.devices.reshape(4, 4, 2, 4), ("y", "z", "core", "x"))
    row = ("y", "z", "core")
    return jax.shard_map(
        body,
        mesh=fine,
        in_specs=(P(row, None), P(row, "x"), P(row, "x")),
        out_specs=(P(row, "x"), P("x", row), P(row, "x")),
        check_vma=False,
    )
```
